256 devices in a mesh: dp: 4 (over x_hi, core), ctx: 64 (over z, x_lo, y).
Axes of the slice: x: 4 (x_hi: 2, x_lo: 2; x = x_hi * 2 + x_lo), y: 4, z: 8, core: 2. Of those that a mesh axis runs over, the one named last changes fastest.
Arguments:
- grad_output: bfloat16 [4, 2048, 8192], P('dp', None, 'ctx'), may hold values from -6 to 6
- post_gate: bfloat16 [4, 2048, 8192], P('dp', None, 'ctx'), may hold values from -6 to 6
- pre_gate: bfloat16 [4, 2048, 8192], P('dp', None, 'ctx'), may hold values from -6 to 6
- value_branch: bfloat16 [4, 2048, 8192], P('dp', None, 'ctx'), may hold values from -6 to 6
- long_filter: float32 [2048, 8192], P('ctx'), may hold values from -0.0625 to 0.0625
- skip_weight: float32 [2048], replicated, may hold values from -3 to 3
Outputs:
- grad_pre_gate: bfloat16 [4, 2048, 8192], P('dp', None, 'ctx')
- grad_value_branch: bfloat16 [4, 2048, 8192], P('dp', None, 'ctx')
- grad_long_filter: float32 [2048, 8192], P('ctx', 'dp')
The draws below stay inside these ranges and needn't reach their ends.
All inputs are finite; a program needn't handle non-finite values.
Results may differ from the reference program's by a relative error of at most 0.0095.
Values may be sent and summed in bfloat16 or wider, within the bound.
A program may use at most 64 MiB of HBM per device.

```python
import math
import jax
import jax.numpy as jnp
from jax import lax

C = 2048
SEQ_LEN = 8192
SEQS = 4
TOKENS = 32768


def shard_levels(key, shape, cuts, low, largest):
    def one(dim, blocks):
        draws = jax.random.uniform(jax.random.fold_in(jax.random.fold_in(key, 6), dim), (blocks,), jnp.float32, low / len(cuts), largest / len(cuts))
        return jnp.repeat(jnp.exp(draws), shape[dim] // blocks).reshape((-1,) + (1,) * (len(shape) - dim - 1))

    factor_of = one(*cuts[0])
    for cut in cuts[1:]:
        factor_of = factor_of * one(*cut)
    return factor_of


def bell_draw(own_key, shape, width, bound, split=(), held_as=jnp.bfloat16):
    values = width * jax.random.normal(own_key, shape, jnp.float32)
    if split:
        values = values * shard_levels(own_key, shape, split, -0.22, 0.18)
    return jnp.clip(values, -bound, bound).astype(held_as)


def setup_inputs(seed: int = 0) -> dict:
    arg_keys = jax.random.split(jax.random.key(seed), 7)
    grad_output = bell_draw(arg_keys[0], (SEQS, C, SEQ_LEN), 1.0, 6.0, ((0, 4), (2, 64)))
    post_gate = bell_draw(arg_keys[1], (SEQS, C, SEQ_LEN), 1.0, 6.0, ((0, 4), (2, 64)))
    pre_gate = bell_draw(arg_keys[2], (SEQS, C, SEQ_LEN), 1.0, 6.0, ((0, 4), (2, 64)))
    value_branch = bell_draw(arg_keys[3], (SEQS, C, SEQ_LEN), 1.0, 6.0, ((0, 4), (2, 64)))
    long_filter = bell_draw(arg_keys[4], (C, SEQ_LEN), SEQ_LEN ** -0.5, 0.0625, ((0, 64),), jnp.float32)
    skip_weight = bell_draw(arg_keys[5], (C,), 1.0, 3.0, (), jnp.float32)
    return dict(grad_output=grad_output, post_gate=post_gate, pre_gate=pre_gate, value_branch=value_branch, long_filter=long_filter, skip_weight=skip_weight)


def reference(grad_output, post_gate, pre_gate, value_branch, long_filter, skip_weight):
    gated = (grad_output.astype(jnp.float32) * post_gate.astype(jnp.float32)).astype(jnp.bfloat16)
    saved = (pre_gate.astype(jnp.float32) * value_branch.astype(jnp.float32)).astype(jnp.bfloat16)
    length = long_filter.shape[1]
    padded = 2 * length

    def per_channel(operands):
        grad_rows, saved_rows, filter_row = operands
        grad_spec = jnp.fft.rfft(grad_rows.astype(jnp.float32), n=padded, axis=-1)
        saved_spec = jnp.fft.rfft(saved_rows.astype(jnp.float32), n=padded, axis=-1)
        filter_spec = jnp.fft.rfft(filter_row, n=padded, axis=-1)
        correlated = jnp.fft.irfft(jnp.conj(filter_spec)[None, :] * grad_spec, n=padded, axis=-1)[:, :length]
        filter_terms = jnp.fft.irfft(grad_spec * jnp.conj(saved_spec), n=padded, axis=-1)[:, :length]
        return (correlated.astype(jnp.bfloat16), lax.optimization_barrier(jnp.sum(filter_terms, axis=0)))
    correlation, filter_sum = lax.map(per_channel, (jnp.swapaxes(gated, 0, 1), jnp.swapaxes(saved, 0, 1), long_filter))
    correlation = jnp.swapaxes(correlation, 0, 1)
    summed = correlation.astype(jnp.float32) + skip_weight[None, :, None] * gated.astype(jnp.float32)
    grad_pre_gate = (summed * value_branch.astype(jnp.float32)).astype(jnp.bfloat16)
    grad_value_branch = (summed * pre_gate.astype(jnp.float32)).astype(jnp.bfloat16)
    grad_long_filter = filter_sum * (1.0 / math.sqrt(TOKENS))
    return (grad_pre_gate, grad_value_branch, grad_long_filter)
```

```python
import functools
import math

import jax
import jax.numpy as jnp
from jax import lax
from jax.experimental import pallas as pl
from jax.experimental.pallas import tpu as pltpu
from jax.sharding import PartitionSpec as P


f32, bf16 = jnp.float32, jnp.bfloat16
B = 128
W = 2048


def row_bits(shape):
    return lax.broadcasted_iota(jnp.int32, shape, 0)


def stagger(v, left):
    width = v.shape[1]
    rows = row_bits(v.shape)
    for bit in (1, 2, 4):
        moved = pltpu.roll(v, (width - bit) if left else bit, 1)
        v = jnp.where((rows & bit) != 0, moved, v)
    return v


def build_filters(fpad, toep):
    length = toep.shape[2]

    @pl.loop(0, 8)
    def _(c):
        @pl.loop(0, length // W)
        def _(w):
            lanes = pl.ds(pl.multiple_of(w * W, W), W + B)
            v = jnp.broadcast_to(fpad[pl.ds(c, 1), lanes], (8, W + B))
            v = stagger(v, False)
            for a in range(0, 16, 2):
                lo = v if a == 0 else pltpu.roll(v, 8 * a, 1)
                hi = pltpu.roll(v, 8 * a + 8, 1)
                both = jnp.concatenate([lo[:, B:], hi[:, B:]], 0).astype(bf16)
                toep[c, pl.ds(8 * a, 16), pl.ds(pl.multiple_of(w * W, W), W)] = both


def shifted(rows, out, c):
    for p in range(4):
        out[c, p, pl.ds(0, 256), :] = rows[pl.ds(c + 32 * p, 256, stride=8), :].astype(bf16)


def correlate(toep, shifts, c):
    acc = jnp.zeros((256, B), f32)
    for d4 in range(16):
        live = 256 - 16 * d4
        part = jnp.zeros((live, B), f32)
        for h in range(2):
            lhs = jnp.concatenate([shifts[c, 2 * h + e, pl.ds(16 * d4, live), :] for e in range(2)], 1)
            rhs = toep[c, :, pl.ds((4 * d4 + 2 * h) * B, 2 * B)]
            part += lax.dot_general(lhs, rhs, (((1,), (1,)), ((), ())), preferred_element_type=f32)
        if live == 256:
            acc += part
        else:
            acc = jnp.concatenate([acc[:live] + part, acc[live:]], 0)
    return acc


PITCH = 136
HALF = 4

def product_blocks(saved_t, shifts, blocks, c, slot):
    for d4 in range(16):
        depth = 256 if d4 < 8 else 128
        for h in range(2):
            m = 4 * d4 + 2 * h
            rhs = jnp.concatenate([shifts[c, 2 * h + e, pl.ds(16 * d4, depth), :] for e in range(2)], 1)
            out = jnp.dot(saved_t[:, :depth], rhs, preferred_element_type=f32)
            for e in range(2):
                blocks[pl.ds(pl.multiple_of((slot * 64 + m + e) * PITCH, 8), B), :] = out[:, e * B:(e + 1) * B]

def fold(blocks, totals, step=8):
    totals[...] = jnp.zeros(totals.shape, f32)
    rows = totals.shape[0]
    k = lax.broadcasted_iota(jnp.int32, (B, 2 * B), 0)
    n = lax.broadcasted_iota(jnp.int32, (B, 2 * B), 1)
    gap = n - k - B

    @pl.loop(0, B // step)
    def _(t):
        lhs, rhs = [], []
        for e in range(step):
            jp = t * step + e
            lhs.append(blocks[pl.ds(jp, rows, stride=PITCH), :].astype(bf16))
            rhs.append(jnp.where(gap == -jp, 1.0, 0.0).astype(bf16))
        totals[...] += jnp.dot(jnp.concatenate(lhs, 1), jnp.concatenate(rhs, 0), preferred_element_type=f32)


def conv_kernel(f_ref, g_ref, s_ref, c_ref, d_ref, fpad, toep, grows, srows, shifts, crows, blocks, totals):
    length = toep.shape[2]
    fpad[:, :B] = jnp.zeros((8, B), f32)
    fpad[:, pl.ds(B, length)] = f_ref[...]
    build_filters(fpad, toep)
    for z in range(8):
        grows[pl.ds(z * 256, 256), :] = g_ref[pl.ds(8 * z, 8)].astype(f32).reshape(256, B)
        srows[pl.ds(z * 256, 256), :] = s_ref[pl.ds(8 * z, 8)].astype(f32).reshape(256, B)
    grows[pl.ds(2048, 128), :] = jnp.zeros((128, B), f32)
    shifts[:, :, pl.ds(256, 128), :] = jnp.zeros((8, 4, 128, B), bf16)

    @pl.loop(0, 8)
    def _(c):
        shifted(grows, shifts, c)
        crows[pl.ds(c, 256, stride=8), :] = correlate(toep, shifts, c)

    for z in range(8):
        c_ref[pl.ds(8 * z, 8)] = crows[pl.ds(z * 256, 256), :].astype(bf16).reshape(8, 4, 8, B)
    for half in range(2):

        @pl.loop(0, HALF)
        def _(q):
            c = half * HALF + q
            saved_t = srows[pl.ds(c, 256, stride=8), :].T.astype(bf16)
            product_blocks(saved_t, shifts, blocks, c, q)

        fold(blocks, totals)
        for q in range(HALF):
            here = totals[pl.ds(64 * q, 64), pl.ds(B, B)]
            later = totals[pl.ds(64 * q, 64), pl.ds(0, B)]
            later = jnp.concatenate([later[1:], jnp.zeros((1, B), f32)], 0)
            d_ref[half * HALF + q] = here + later


def conv(f, g, s):
    length = f.shape[1]
    vm = pl.BlockSpec(memory_space=pltpu.VMEM)
    return pl.pallas_call(
        conv_kernel,
        out_shape=(jax.ShapeDtypeStruct(g.shape, bf16), jax.ShapeDtypeStruct((8, 64, B), f32)),
        in_specs=[vm] * 3,
        out_specs=(vm, vm),
        scratch_shapes=[
            pltpu.VMEM((8, length + B), f32),
            pltpu.VMEM((8, B, length), bf16),
            pltpu.VMEM((2048 + 128, B), f32),
            pltpu.VMEM((2048, B), f32),
            pltpu.VMEM((8, 4, 384, B), bf16),
            pltpu.VMEM((2048, B), f32),
            pltpu.VMEM((HALF * 64 * PITCH, B), f32),
            pltpu.VMEM((HALF * 64, 2 * B), f32),
        ],
        compiler_params=pltpu.CompilerParams(vmem_limit_bytes=60 << 20),
        name="conv",
    )(f, g, s)


def exchange(blocks, axes):
    return lax.all_to_all(blocks, axes, split_axis=0, concat_axis=0, tiled=True)


def shards(grad_output, post_gate, pre_gate, value_branch, long_filter, skip_weight):
    token_count = 4 * long_filter.shape[1]
    gated = (grad_output.astype(f32) * post_gate.astype(f32)).astype(bf16)
    saved = (pre_gate.astype(f32) * value_branch.astype(f32)).astype(bf16)
    own = lax.dynamic_slice_in_dim(long_filter, lax.axis_index("dp") * 8, 8, 0)
    axes = ("ctx", "dp")
    g = exchange(gated.reshape(256, 8, B), axes).reshape(64, 4, 8, B)
    s = exchange(saved.reshape(256, 8, B), axes).reshape(64, 4, 8, B)
    c, d = conv(own, g, s)
    back = exchange(c.reshape(256, 8, B), axes).reshape(1, 2048, B)
    d = d.reshape(8, 4, 2048).swapaxes(0, 1).reshape(32, 2048).astype(bf16)
    shares = lax.all_to_all(d, "dp", split_axis=0, concat_axis=0, tiled=True).astype(f32)
    summed = back.astype(f32) + skip_weight[None, :, None] * gated.astype(f32)
    return (
        (summed * value_branch.astype(f32)).astype(bf16),
        (summed * pre_gate.astype(f32)).astype(bf16),
        shares * (1.0 / math.sqrt(token_count)),
    )


def solution(mesh):
    return jax.shard_map(
        shards,
        mesh=mesh,
        in_specs=(P("dp", None, "ctx"),) * 4 + (P("ctx", None), P()),
        out_specs=(P("dp", None, "ctx"), P("dp", None, "ctx"), P("ctx", "dp")),
        check_vma=False,
    )
```

```python
import functools
import math

import jax
import jax.numpy as jnp
from jax import lax
from jax.experimental import pallas as pl
from jax.experimental.pallas import tpu as pltpu
from jax.sharding import PartitionSpec as P

MESH = pl.DeviceIdType.MESH
ORDER = (4, 3, 5, 6, 2, 7, 1, 0)
GROUPS = ((0, 4), (4, 4))

f32, bf16 = jnp.float32, jnp.bfloat16
B = 128
W = 2048


def row_bits(shape):
    return lax.broadcasted_iota(jnp.int32, shape, 0)


def stagger(v, left):
    width = v.shape[1]
    rows = row_bits(v.shape)
    for bit in (1, 2, 4):
        moved = pltpu.roll(v, (width - bit) if left else bit, 1)
        v = jnp.where((rows & bit) != 0, moved, v)
    return v


def build_filters(fpad, toep, first, last):
    length = toep.shape[2]

    @pl.loop(first, last)
    def _(c):
        @pl.loop(0, length // W)
        def _(w):
            lanes = pl.ds(pl.multiple_of(w * W, W), W + B)
            v = jnp.broadcast_to(fpad[pl.ds(c, 1), lanes], (8, W + B))
            v = stagger(v, False)
            for a in range(0, 16, 2):
                lo = v if a == 0 else pltpu.roll(v, 8 * a, 1)
                hi = pltpu.roll(v, 8 * a + 8, 1)
                both = jnp.concatenate([lo[:, B:], hi[:, B:]], 0).astype(bf16)
                toep[c, pl.ds(8 * a, 16), pl.ds(pl.multiple_of(w * W, W), W)] = both


def shifted(rows, out, c):
    for p in range(4):
        out[c, p, pl.ds(0, 256), :] = rows[pl.ds(c + 32 * p, 256, stride=8), :].astype(bf16)


def correlate(toep, shifts, c):
    acc = jnp.zeros((256, B), f32)
    for d4 in range(16):
        live = 256 - 16 * d4
        part = jnp.zeros((live, B), f32)
        for h in range(2):
            lhs = jnp.concatenate([shifts[c, 2 * h + e, pl.ds(16 * d4, live), :] for e in range(2)], 1)
            rhs = toep[c, :, pl.ds((4 * d4 + 2 * h) * B, 2 * B)]
            part += lax.dot_general(lhs, rhs, (((1,), (1,)), ((), ())), preferred_element_type=f32)
        if live == 256:
            acc += part
        else:
            acc = jnp.concatenate([acc[:live] + part, acc[live:]], 0)
    return acc


PITCH = 136
HALF = 4

def product_blocks(saved_t, shifts, blocks, c, slot):
    for d4 in range(16):
        depth = 256 if d4 < 8 else 128
        for h in range(2):
            m = 4 * d4 + 2 * h
            rhs = jnp.concatenate([shifts[c, 2 * h + e, pl.ds(16 * d4, depth), :] for e in range(2)], 1)
            out = jnp.dot(saved_t[:, :depth], rhs, preferred_element_type=f32)
            for e in range(2):
                blocks[pl.ds(pl.multiple_of((slot * 64 + m + e) * PITCH, 8), B), :] = out[:, e * B:(e + 1) * B]

def fold(blocks, totals, step=8):
    totals[...] = jnp.zeros(totals.shape, f32)
    rows = totals.shape[0]
    k = lax.broadcasted_iota(jnp.int32, (B, 2 * B), 0)
    n = lax.broadcasted_iota(jnp.int32, (B, 2 * B), 1)
    gap = n - k - B

    @pl.loop(0, B // step)
    def _(t):
        lhs, rhs = [], []
        for e in range(step):
            jp = t * step + e
            lhs.append(blocks[pl.ds(jp, rows, stride=PITCH), :].astype(bf16))
            rhs.append(jnp.where(gap == -jp, 1.0, 0.0).astype(bf16))
        totals[...] += jnp.dot(jnp.concatenate(lhs, 1), jnp.concatenate(rhs, 0), preferred_element_type=f32)


def wrap(v, n):
    return jnp.where(v >= n, v - n, v)


def kernel(
    go_hbm, pg_hbm, pre_hbm, val_hbm, filt_hbm, skip_ref, gp_ref, gv_ref, taps_ref,
    go, pg, pre, val, g_own, s_own, g_z, s_z, g_all, s_all, c_own, c_xy, c_z, t_own, t_all,
    fpad, toep, grows, srows, shifts, crows, blocks, totals, trows, direct,
    load_sem, z_send, z_recv, xy_send, xy_recv, t_send, t_recv,
):
    length = toep.shape[2]
    dp, ctx = lax.axis_index("dp"), lax.axis_index("ctx")
    z = ctx // 8
    plane = ctx - 8 * z
    xl = plane // 4
    y = plane - 4 * xl
    xh = dp // 2
    core = dp - 2 * xh
    x = 2 * xh + xl
    q = plane * 4 + dp

    def z_peer(k, back):
        step = ORDER[k] if back else (8 - ORDER[k]) % 8
        return wrap(z + step, 8)

    def each_xy_peer(body):
        @pl.loop(0, 4)
        def _(dy):
            y2 = wrap(y + dy, 4)
            for dx in range(4):
                x2 = wrap(x + dx, 4)
                xh2 = jnp.where(x2 >= 2, 1, 0)
                plane2 = (x2 - 2 * xh2) * 4 + y2
                for dc in range(2):
                    core2 = wrap(core + dc, 2)
                    dp2 = 2 * xh2 + core2
                    if dx or dc:
                        body(dp2, z * 8 + plane2, plane2 * 4 + dp2)
                    else:

                        @pl.when(dy > 0)
                        def _():
                            body(dp2, z * 8 + plane2, plane2 * 4 + dp2)

    barrier = pltpu.get_barrier_semaphore()
    for k in range(7):
        pl.semaphore_signal(
            barrier, inc=1, device_id=(dp, z_peer(k, False) * 8 + plane), device_id_type=MESH
        )
    each_xy_peer(
        lambda d, c, q2: pl.semaphore_signal(barrier, inc=1, device_id=(d, c), device_id_type=MESH)
    )
    loads = [
        pltpu.make_async_copy(a, b, load_sem.at[n])
        for n, (a, b) in enumerate(
            (
                (go_hbm, go), (pg_hbm, pg), (pre_hbm, pre), (val_hbm, val),
                (filt_hbm.at[pl.ds(pl.multiple_of(8 * dp, 8), 8)], fpad.at[:, pl.ds(B, length)]),
            )
        )
    ]
    for load in loads:
        load.start()

    def elementwise(a, b, out):
        @pl.loop(0, 8)
        def _(n):
            rows = pl.ds(pl.multiple_of(n * 256, 256), 256)
            prod = (a[rows, :].astype(f32) * b[rows, :].astype(f32)).astype(bf16)
            out[n] = prod.reshape(32, 8, B)

    def z_sends(src, dst, n):
        return [
            pltpu.make_async_remote_copy(
                src_ref=src.at[z_peer(k, False)], dst_ref=dst.at[k],
                send_sem=z_send.at[n, k], recv_sem=z_recv.at[n, k],
                device_id=(dp, z_peer(k, False) * 8 + plane), device_id_type=MESH,
            )
            for k in range(7)
        ]

    def xy_start(src, dst, n, g, out):
        lo, count = GROUPS[g]

        def one(d, c, q2):
            slots = pl.ds(lo, count)
            pltpu.make_async_remote_copy(
                src_ref=src.at[q2, slots] if out else src.at[slots, q2],
                dst_ref=dst.at[q, slots],
                send_sem=xy_send.at[n, g], recv_sem=xy_recv.at[n, g],
                device_id=(d, c), device_id_type=MESH,
            ).start()

        each_xy_peer(one)

    def xy_wait(src, dst, n, g, out, send):
        slots = pl.ds(*GROUPS[g])
        if send:
            part = src.at[pl.ds(0, 31), slots] if out else src.at[slots, pl.ds(0, 31)]
            pltpu.make_async_copy(part, part, xy_send.at[n, g]).wait()
        else:
            part = dst.at[pl.ds(0, 31), slots]
            pltpu.make_async_copy(part, part, xy_recv.at[n, g]).wait()

    loads[0].wait()
    loads[1].wait()
    elementwise(go, pg, g_own)
    pl.semaphore_wait(barrier, 38)
    g_sends = z_sends(g_own, g_z, 0)
    for send in g_sends:
        send.start()
    g_z[7] = g_own[z]
    loads[2].wait()
    loads[3].wait()
    elementwise(pre, val, s_own)
    s_z[7] = s_own[z]
    s_sends = z_sends(s_own, s_z, 1)

    skip_t = skip_ref[...].T
    for n in range(16):
        part = g_own[n // 2, pl.ds(16 * (n % 2), 16)].astype(f32).reshape(B, B)
        direct[pl.ds(n * B, B), :] = part * skip_t[:, n : n + 1]

    loads[4].wait()
    fpad[:, :B] = jnp.zeros((8, B), f32)
    grows[pl.ds(2048, 128), :] = jnp.zeros((128, B), f32)
    shifts[:, :, pl.ds(256, 128), :] = jnp.zeros((8, 4, 128, B), bf16)
    build_filters(fpad, toep, 0, 3)
    for k in range(4):
        g_sends[k].wait_recv()
    xy_start(g_z, g_all, 0, 0, False)
    for send in s_sends:
        send.start()
    build_filters(fpad, toep, 3, 4)
    for k in range(4, 7):
        g_sends[k].wait_recv()
    xy_start(g_z, g_all, 0, 1, False)
    for k in range(8):
        g_all[q, k] = g_z[k, q]
    build_filters(fpad, toep, 4, 8)

    def unpack(slabs, rows):
        for k in range(8):
            there = wrap(z + ORDER[k], 8)
            rows[pl.ds(pl.multiple_of(there * 256, 256), 256), :] = (
                slabs[:, k].astype(f32).reshape(256, B)
            )

    xy_wait(g_z, g_all, 0, 0, False, False)
    xy_wait(g_z, g_all, 0, 1, False, False)
    unpack(g_all, grows)

    @pl.loop(0, 8)
    def _(c):
        shifted(grows, shifts, c)
        crows[pl.ds(c, 256, stride=8), :] = correlate(toep, shifts, c)

    for k in range(8):
        there = wrap(z + ORDER[k], 8)
        c_own[:, k] = (
            crows[pl.ds(pl.multiple_of(there * 256, 256), 256), :].astype(bf16).reshape(32, 8, B)
        )
    xy_start(c_own, c_xy, 2, 0, True)
    xy_start(c_own, c_xy, 2, 1, True)
    for k in range(8):
        c_xy[q, k] = c_own[q, k]

    for k in range(4):
        s_sends[k].wait_recv()
    xy_start(s_z, s_all, 1, 0, False)
    for k in range(4, 7):
        s_sends[k].wait_recv()
    xy_start(s_z, s_all, 1, 1, False)
    for k in range(8):
        s_all[q, k] = s_z[k, q]

    c_sends = [
        pltpu.make_async_remote_copy(
            src_ref=c_xy.at[:, k], dst_ref=c_z.at[k],
            send_sem=z_send.at[2, k], recv_sem=z_recv.at[2, k],
            device_id=(dp, z_peer(k, True) * 8 + plane), device_id_type=MESH,
        )
        for k in range(7)
    ]
    for g in range(2):
        xy_wait(c_own, c_xy, 2, g, True, False)
        for k in range(GROUPS[g][0], min(7, sum(GROUPS[g]))):
            c_sends[k].start()
    c_z[7] = c_xy[:, 7]

    xy_wait(s_z, s_all, 1, 0, False, False)
    xy_wait(s_z, s_all, 1, 1, False, False)
    unpack(s_all, srows)
    for half in range(2):

        @pl.loop(0, HALF)
        def _(n):
            c = half * HALF + n
            saved_t = srows[pl.ds(c, 256, stride=8), :].T.astype(bf16)
            product_blocks(saved_t, shifts, blocks, c, n)

        fold(blocks, totals)
        for n in range(HALF):
            here = totals[pl.ds(64 * n, 64), pl.ds(B, B)]
            later = totals[pl.ds(64 * n, 64), pl.ds(0, B)]
            later = jnp.concatenate([later[1:], jnp.zeros((1, B), f32)], 0)
            trows[pl.ds(half * HALF + n, 64, stride=8), :] = here + later

    for p in range(4):
        t_own[p] = trows[pl.ds(128 * p, 128), :].astype(bf16).reshape(16, 8, B)
    t_sends = []
    for s in range(1, 4):
        p = wrap(dp + s, 4)
        t_sends.append(
            pltpu.make_async_remote_copy(
                src_ref=t_own.at[p], dst_ref=t_all.at[s],
                send_sem=t_send.at[s - 1], recv_sem=t_recv.at[s - 1],
                device_id=(p, ctx), device_id_type=MESH,
            )
        )
        t_sends[-1].start()
    t_all[0] = t_own[dp]

    for k in (7, 0, 1, 2, 3, 4, 5, 6):
        if k < 7:
            c_sends[k].wait_recv()
        rows = pl.ds(pl.multiple_of(z_peer(k, False) * 256, 256), 256)
        summed = c_z[k].astype(f32).reshape(256, B) + direct[rows, :]
        gp_ref[rows, :] = (summed * val[rows, :].astype(f32)).astype(bf16)
        gv_ref[rows, :] = (summed * pre[rows, :].astype(f32)).astype(bf16)

    scale = 1.0 / math.sqrt(4 * length)
    for s in range(4):
        if s:
            t_sends[s - 1].wait_recv()
        rows = pl.ds(pl.multiple_of(8 * wrap(dp + (4 - s) % 4, 4), 8), 8)
        for m in range(16):
            taps_ref[rows, pl.ds(m * B, B)] = t_all[s, m].astype(f32) * scale

    for send in g_sends + s_sends + c_sends + t_sends:
        send.wait_send()
    for g in range(2):
        xy_wait(g_z, g_all, 0, g, False, True)
        xy_wait(s_z, s_all, 1, g, False, True)
        xy_wait(c_own, c_xy, 2, g, True, True)


def shards(grad_output, post_gate, pre_gate, value_branch, long_filter, skip_weight):
    channels, length = skip_weight.shape[0], long_filter.shape[1]
    vm = pl.BlockSpec(memory_space=pltpu.VMEM)
    own = pltpu.VMEM((channels, B), bf16)
    by_z = pltpu.VMEM((8, 32, 8, B), bf16)
    by_q = pltpu.VMEM((32, 8, 8, B), bf16)
    by_p = pltpu.VMEM((4, 16, 8, B), bf16)
    dma = pltpu.SemaphoreType.DMA
    gp, gv, taps = pl.pallas_call(
        kernel,
        out_shape=(
            jax.ShapeDtypeStruct((channels, B), bf16),
            jax.ShapeDtypeStruct((channels, B), bf16),
            jax.ShapeDtypeStruct((32, length // 4), f32),
        ),
        in_specs=[pl.BlockSpec(memory_space=pl.ANY)] * 5 + [vm],
        out_specs=(vm, vm, vm),
        scratch_shapes=[own] * 4
        + [by_z] * 4
        + [by_q] * 4
        + [by_z]
        + [by_p] * 2
        + [
            pltpu.VMEM((8, length + B), f32),
            pltpu.VMEM((8, B, length), bf16),
            pltpu.VMEM((2048 + 128, B), f32),
            pltpu.VMEM((2048, B), f32),
            pltpu.VMEM((8, 4, 384, B), bf16),
            pltpu.VMEM((2048, B), f32),
            pltpu.VMEM((HALF * 64 * PITCH, B), f32),
            pltpu.VMEM((HALF * 64, 2 * B), f32),
            pltpu.VMEM((512, B), f32),
            pltpu.VMEM((2048, B), f32),
            dma((5,)),
            dma((3, 7)),
            dma((3, 7)),
            dma((3, 2)),
            dma((3, 2)),
            dma((3,)),
            dma((3,)),
        ],
        compiler_params=pltpu.CompilerParams(
            collective_id=0, has_side_effects=True, vmem_limit_bytes=62 << 20
        ),
        name="hyena",
    )(
        grad_output[0], post_gate[0], pre_gate[0], value_branch[0], long_filter,
        skip_weight.reshape(16, B),
    )
    return gp[None], gv[None], taps


def solution(mesh):
    return jax.shard_map(
        shards,
        mesh=mesh,
        in_specs=(P("dp", None, "ctx"),) * 4 + (P("ctx", None), P()),
        out_specs=(P("dp", None, "ctx"), P("dp", None, "ctx"), P("ctx", "dp")),
        check_vma=False,
    )
```

```python
import functools
import math

import jax
import jax.numpy as jnp
from jax import lax
from jax.experimental import pallas as pl
from jax.experimental.pallas import tpu as pltpu
from jax.sharding import PartitionSpec as P

MESH = pl.DeviceIdType.MESH
ORDER = (4, 3, 5, 6, 2, 7, 1, 0)
AHEAD = 2

f32, bf16 = jnp.float32, jnp.bfloat16
B = 128
W = 2048


def row_bits(shape):
    return lax.broadcasted_iota(jnp.int32, shape, 0)


def stagger(v, left):
    width = v.shape[1]
    rows = row_bits(v.shape)
    for bit in (1, 2, 4):
        moved = pltpu.roll(v, (width - bit) if left else bit, 1)
        v = jnp.where((rows & bit) != 0, moved, v)
    return v


def build_filters(fpad, toep, first, last):
    length = toep.shape[2]

    @pl.loop(first, last)
    def _(c):
        @pl.loop(0, length // W)
        def _(w):
            lanes = pl.ds(pl.multiple_of(w * W, W), W + B)
            v = jnp.broadcast_to(fpad[pl.ds(c, 1), lanes], (8, W + B))
            v = stagger(v, False)
            for a in range(0, 16, 2):
                lo = v if a == 0 else pltpu.roll(v, 8 * a, 1)
                hi = pltpu.roll(v, 8 * a + 8, 1)
                both = jnp.concatenate([lo[:, B:], hi[:, B:]], 0).astype(bf16)
                toep[c, pl.ds(8 * a, 16), pl.ds(pl.multiple_of(w * W, W), W)] = both


def shifted(rows, out, c):
    for p in range(4):
        out[c, p, pl.ds(0, 256), :] = rows[pl.ds(c + 32 * p, 256, stride=8), :].astype(bf16)


def correlate(toep, shifts, c):
    acc = jnp.zeros((256, B), f32)
    for d4 in range(16):
        live = 256 - 16 * d4
        part = jnp.zeros((live, B), f32)
        for h in range(2):
            lhs = jnp.concatenate([shifts[c, 2 * h + e, pl.ds(16 * d4, live), :] for e in range(2)], 1)
            rhs = toep[c, :, pl.ds((4 * d4 + 2 * h) * B, 2 * B)]
            part += lax.dot_general(lhs, rhs, (((1,), (1,)), ((), ())), preferred_element_type=f32)
        if live == 256:
            acc += part
        else:
            acc = jnp.concatenate([acc[:live] + part, acc[live:]], 0)
    return acc


PITCH = 136
HALF = 4

def product_blocks(saved_t, shifts, blocks, c, slot):
    for d4 in range(16):
        depth = 256 if d4 < 8 else 128
        for h in range(2):
            m = 4 * d4 + 2 * h
            rhs = jnp.concatenate([shifts[c, 2 * h + e, pl.ds(16 * d4, depth), :] for e in range(2)], 1)
            out = jnp.dot(saved_t[:, :depth], rhs, preferred_element_type=f32)
            for e in range(2):
                blocks[pl.ds(pl.multiple_of((slot * 64 + m + e) * PITCH, 8), B), :] = out[:, e * B:(e + 1) * B]

def fold(blocks, totals, step=16):
    totals[...] = jnp.zeros(totals.shape, f32)
    rows = totals.shape[0]
    k = lax.broadcasted_iota(jnp.int32, (B, 2 * B), 0)
    n = lax.broadcasted_iota(jnp.int32, (B, 2 * B), 1)
    gap = n - k - B

    @pl.loop(0, B // step)
    def _(t):
        lhs, rhs = [], []
        for e in range(step):
            jp = t * step + e
            lhs.append(blocks[pl.ds(jp, rows, stride=PITCH), :].astype(bf16))
            rhs.append(jnp.where(gap == -jp, 1.0, 0.0).astype(bf16))
        totals[...] += jnp.dot(jnp.concatenate(lhs, 1), jnp.concatenate(rhs, 0), preferred_element_type=f32)


def wrap(v, n):
    return jnp.where(v >= n, v - n, v)


def kernel(
    go_hbm, pg_hbm, pre_hbm, val_hbm, filt_hbm, back_ref, taps_ref,
    go, pg, pre, val, g_own, s_own, g_z, s_z, g_all, s_all, c_own, c_xy, c_z, t_own, t_all,
    fpad, toep, grows, srows, shifts, crows, blocks, totals, trows,
    load_sem, z_send, z_recv, xy_send, xy_recv, c_recv, t_send, t_recv,
):
    length = toep.shape[2]
    dp, ctx = lax.axis_index("dp"), lax.axis_index("ctx")
    z = ctx // 8
    plane = ctx - 8 * z
    xl = plane // 4
    y = plane - 4 * xl
    xh = dp // 2
    core = dp - 2 * xh
    x = 2 * xh + xl
    q = plane * 4 + dp
    member = plane * 2 + xh

    loads = [
        pltpu.make_async_copy(a, b, load_sem.at[n])
        for n, (a, b) in enumerate(
            (
                (go_hbm, go), (pg_hbm, pg), (pre_hbm, pre), (val_hbm, val),
                (filt_hbm.at[pl.ds(pl.multiple_of(8 * dp, 8), 8)], fpad.at[:, pl.ds(B, length)]),
            )
        )
    ]
    for load in loads:
        load.start()

    def z_peer(k, back):
        step = ORDER[k] if back else (8 - ORDER[k]) % 8
        return wrap(z + step, 8)

    def chip(x2, y2):
        xh2 = jnp.where(x2 >= 2, 1, 0)
        return (x2 - 2 * xh2) * 4 + y2, xh2

    def each_xy_peer(body):
        @pl.loop(0, 4)
        def _(dy):
            y2 = wrap(y + dy, 4)
            for dx in range(4):
                plane2, xh2 = chip(wrap(x + dx, 4), y2)
                for dc in range(2):
                    dp2 = 2 * xh2 + wrap(core + dc, 2)
                    if dx or dc:
                        body(dp2, z * 8 + plane2, plane2 * 4 + dp2)
                    else:

                        @pl.when(dy > 0)
                        def _():
                            body(dp2, z * 8 + plane2, plane2 * 4 + dp2)

    barrier = pltpu.get_barrier_semaphore()
    for k in range(7):
        pl.semaphore_signal(
            barrier, inc=1, device_id=(dp, z_peer(k, False) * 8 + plane), device_id_type=MESH
        )
    each_xy_peer(
        lambda d, c, q2: pl.semaphore_signal(barrier, inc=1, device_id=(d, c), device_id_type=MESH)
    )

    def elementwise(a, b, out):
        @pl.loop(0, 8)
        def _(there):
            rows = pl.ds(pl.multiple_of(there * 256, 256), 256)
            prod = (a[rows, :].astype(f32) * b[rows, :].astype(f32)).reshape(16, 2, 8, B)
            for n in range(2):
                out[n, there] = prod[:, n].astype(bf16)

    def z_sends(src, dst, t, n):
        return [
            pltpu.make_async_remote_copy(
                src_ref=src.at[n, z_peer(k, False)], dst_ref=dst.at[n, k],
                send_sem=z_send.at[t, n, k], recv_sem=z_recv.at[t, n, k],
                device_id=(dp, z_peer(k, False) * 8 + plane), device_id_type=MESH,
            )
            for k in range(7)
        ]

    def spread(src, dst, t, n):
        @pl.loop(0, 4)
        def _(dy):
            y2 = wrap(y + dy, 4)
            for dx in range(4):
                plane2, xh2 = chip(wrap(x + dx, 4), y2)
                copy = pltpu.make_async_remote_copy(
                    src_ref=src.at[n, :, plane2 * 2 + xh2], dst_ref=dst.at[q],
                    send_sem=xy_send.at[t], recv_sem=xy_recv.at[t],
                    device_id=(2 * xh2 + n, z * 8 + plane2), device_id_type=MESH,
                )
                if dx:
                    copy.start()
                else:
                    pl.when((dy > 0) | (core != n))(copy.start)

    def wait_31(ref, sem):
        part = ref.at[pl.ds(0, 31)]
        pltpu.make_async_copy(part, part, sem).wait()

    loads[0].wait()
    loads[1].wait()
    elementwise(go, pg, g_own)
    pl.semaphore_wait(barrier, 38)
    g_sends = [z_sends(g_own, g_z, 0, n) for n in range(2)]
    s_sends = [z_sends(s_own, s_z, 1, n) for n in range(2)]
    queue = g_sends + s_sends

    def launch(n):
        if n < 4:
            for send in queue[n]:
                send.start()

    def forward(n):
        for send in queue[n]:
            send.wait_recv()
        launch(n + AHEAD)
        if n < 2:
            spread(g_z, g_all, 0, n)
        else:
            spread(s_z, s_all, 1, n - 2)

    for n in range(AHEAD):
        launch(n)
    for n in range(2):
        g_z[n, 7] = g_own[n, z]
    loads[2].wait()
    loads[3].wait()
    elementwise(pre, val, s_own)
    for n in range(2):
        s_z[n, 7] = s_own[n, z]

    loads[4].wait()
    fpad[:, :B] = jnp.zeros((8, B), f32)
    grows[pl.ds(2048, 128), :] = jnp.zeros((128, B), f32)
    shifts[:, :, pl.ds(256, 128), :] = jnp.zeros((8, 4, 128, B), bf16)
    build_filters(fpad, toep, 0, 3)
    forward(0)
    build_filters(fpad, toep, 3, 6)
    forward(1)
    g_all[q] = g_z[core, :, member]
    build_filters(fpad, toep, 6, 8)

    def unpack(slabs, rows):
        for k in range(8):
            there = wrap(z + ORDER[k], 8)
            rows[pl.ds(pl.multiple_of(there * 256, 256), 256), :] = (
                slabs[:, k].astype(f32).reshape(256, B)
            )

    wait_31(g_all, xy_recv.at[0])
    unpack(g_all, grows)

    def correlations(first, last):
        @pl.loop(first, last)
        def _(c):
            shifted(grows, shifts, c)
            crows[pl.ds(c, 256, stride=8), :] = correlate(toep, shifts, c)

    correlations(0, 3)
    forward(2)
    correlations(3, 6)
    forward(3)
    s_all[q] = s_z[core, :, member]
    correlations(6, 8)

    for k in range(8):
        there = wrap(z + ORDER[k], 8)
        c_own[:, k] = (
            crows[pl.ds(pl.multiple_of(there * 256, 256), 256), :].astype(bf16).reshape(32, 8, B)
        )

    def back(d, c, q2):
        pltpu.make_async_remote_copy(
            src_ref=c_own.at[q2], dst_ref=c_xy.at[core, member],
            send_sem=xy_send.at[2], recv_sem=c_recv.at[core],
            device_id=(d, c), device_id_type=MESH,
        ).start()

    each_xy_peer(back)
    c_xy[core, member] = c_own[q]

    c_sends = [
        pltpu.make_async_remote_copy(
            src_ref=c_xy.at[n, :, k], dst_ref=c_z.at[k, n],
            send_sem=z_send.at[2, n, k], recv_sem=z_recv.at[2, n, k],
            device_id=(dp, z_peer(k, True) * 8 + plane), device_id_type=MESH,
        )
        for n in range(2)
        for k in range(7)
    ]

    def part_wait(n, count):
        part = c_xy.at[n, pl.ds(0, count)]
        pltpu.make_async_copy(part, part, c_recv.at[n]).wait()

    def send_back(n):
        pl.when(core == n)(lambda: part_wait(n, 15))
        pl.when(core != n)(lambda: part_wait(n, 16))
        for send in c_sends[7 * n : 7 * n + 7]:
            send.start()
        c_z[7, n] = c_xy[n, :, 7]

    def multiply(first, last, base):
        @pl.loop(first, last)
        def _(c):
            saved_t = srows[pl.ds(c, 256, stride=8), :].T.astype(bf16)
            product_blocks(saved_t, shifts, blocks, c, c - base)

    def sum_up(base):
        fold(blocks, totals)
        for n in range(HALF):
            here = totals[pl.ds(64 * n, 64), pl.ds(B, B)]
            later = totals[pl.ds(64 * n, 64), pl.ds(0, B)]
            later = jnp.concatenate([later[1:], jnp.zeros((1, B), f32)], 0)
            trows[pl.ds(base + n, 64, stride=8), :] = here + later

    wait_31(s_all, xy_recv.at[1])
    unpack(s_all, srows)
    multiply(0, 3, 0)
    send_back(0)
    multiply(3, 4, 0)
    send_back(1)
    sum_up(0)
    multiply(4, 8, 4)
    sum_up(4)

    for p in range(4):
        t_own[p] = trows[pl.ds(128 * p, 128), :].astype(bf16).reshape(16, 8, B)
    t_sends = []
    for s in range(1, 4):
        p = wrap(dp + s, 4)
        t_sends.append(
            pltpu.make_async_remote_copy(
                src_ref=t_own.at[p], dst_ref=t_all.at[s],
                send_sem=t_send.at[s - 1], recv_sem=t_recv.at[s - 1],
                device_id=(p, ctx), device_id_type=MESH,
            )
        )
        t_sends[-1].start()
    t_all[0] = t_own[dp]

    for send in c_sends:
        send.wait_recv()
    for k in range(8):
        for n in range(2):
            for m in range(16):
                back_ref[z_peer(k, False), 2 * m + n] = c_z[k, n, m]

    for s in range(4):
        if s:
            t_sends[s - 1].wait_recv()
        rows = pl.ds(pl.multiple_of(8 * wrap(dp + (4 - s) % 4, 4), 8), 8)
        for m in range(16):
            taps_ref[rows, pl.ds(m * B, B)] = t_all[s, m].astype(f32)

    for send in sum(queue, []) + c_sends + t_sends:
        send.wait_send()
    wait_31(g_all, xy_send.at[0])
    wait_31(s_all, xy_send.at[1])
    wait_31(c_own, xy_send.at[2])


def shards(grad_output, post_gate, pre_gate, value_branch, long_filter, skip_weight):
    channels, length = skip_weight.shape[0], long_filter.shape[1]
    vm = pl.BlockSpec(memory_space=pltpu.VMEM)
    own = pltpu.VMEM((channels, B), bf16)
    by_class = pltpu.VMEM((2, 8, 16, 8, B), bf16)
    by_q = pltpu.VMEM((32, 8, 8, B), bf16)
    by_p = pltpu.VMEM((4, 16, 8, B), bf16)
    dma = pltpu.SemaphoreType.DMA
    back, taps = pl.pallas_call(
        kernel,
        out_shape=(
            jax.ShapeDtypeStruct((8, 32, 8, B), bf16),
            jax.ShapeDtypeStruct((32, length // 4), f32),
        ),
        in_specs=[pl.BlockSpec(memory_space=pl.ANY)] * 5,
        out_specs=(vm, vm),
        scratch_shapes=[own] * 4
        + [by_class] * 4
        + [by_q] * 3
        + [pltpu.VMEM((2, 16, 8, 8, B), bf16), pltpu.VMEM((8, 2, 16, 8, B), bf16)]
        + [by_p] * 2
        + [
            pltpu.VMEM((8, length + B), f32),
            pltpu.VMEM((8, B, length), bf16),
            pltpu.VMEM((2048 + 128, B), f32),
            pltpu.VMEM((2048, B), f32),
            pltpu.VMEM((8, 4, 384, B), bf16),
            pltpu.VMEM((2048, B), f32),
            pltpu.VMEM((HALF * 64 * PITCH, B), f32),
            pltpu.VMEM((HALF * 64, 2 * B), f32),
            pltpu.VMEM((512, B), f32),
            dma((5,)),
            dma((3, 2, 7)),
            dma((3, 2, 7)),
            dma((3,)),
            dma((2,)),
            dma((2,)),
            dma((3,)),
            dma((3,)),
        ],
        compiler_params=pltpu.CompilerParams(
            collective_id=0, has_side_effects=True, vmem_limit_bytes=62 << 20
        ),
        name="hyena",
    )(grad_output[0], post_gate[0], pre_gate[0], value_branch[0], long_filter)
    gated = (grad_output.astype(f32) * post_gate.astype(f32)).astype(bf16)
    summed = back.reshape(1, channels, B).astype(f32) + skip_weight[None, :, None] * gated.astype(f32)
    return (
        (summed * value_branch.astype(f32)).astype(bf16),
        (summed * pre_gate.astype(f32)).astype(bf16),
        taps * (1.0 / math.sqrt(4 * length)),
    )


def solution(mesh):
    return jax.shard_map(
        shards,
        mesh=mesh,
        in_specs=(P("dp", None, "ctx"),) * 4 + (P("ctx", None), P()),
        out_specs=(P("dp", None, "ctx"), P("dp", None, "ctx"), P("ctx", "dp")),
        check_vma=False,
    )
```

```python
import functools
import math

import jax
import jax.numpy as jnp
from jax import lax
from jax.experimental import pallas as pl
from jax.experimental.pallas import tpu as pltpu
from jax.sharding import PartitionSpec as P

MESH = pl.DeviceIdType.MESH
ORDER = (4, 3, 5, 6, 2, 7, 1, 0)
AHEAD = 2

f32, bf16 = jnp.float32, jnp.bfloat16
B = 128
W = 2048


def row_bits(shape):
    return lax.broadcasted_iota(jnp.int32, shape, 0)


def stagger(v, left):
    width = v.shape[1]
    rows = row_bits(v.shape)
    for bit in (1, 2, 4):
        moved = pltpu.roll(v, (width - bit) if left else bit, 1)
        v = jnp.where((rows & bit) != 0, moved, v)
    return v


def build_filters(fpad, toep, first, last):
    length = toep.shape[2]

    @pl.loop(first, last)
    def _(c):
        @pl.loop(0, length // W)
        def _(w):
            lanes = pl.ds(pl.multiple_of(w * W, W), W + B)
            v = jnp.broadcast_to(fpad[pl.ds(c, 1), lanes], (8, W + B))
            v = stagger(v, False)
            for a in range(0, 16, 2):
                lo = v if a == 0 else pltpu.roll(v, 8 * a, 1)
                hi = pltpu.roll(v, 8 * a + 8, 1)
                both = jnp.concatenate([lo[:, B:], hi[:, B:]], 0).astype(bf16)
                toep[c, pl.ds(8 * a, 16), pl.ds(pl.multiple_of(w * W, W), W)] = both


def shifted(rows, out, c):
    for p in range(4):
        out[c, p, pl.ds(0, 256), :] = rows[pl.ds(c + 32 * p, 256, stride=8), :].astype(bf16)


def correlate(toep, shifts, c):
    acc = jnp.zeros((256, B), f32)
    for d4 in range(16):
        live = 256 - 16 * d4
        part = jnp.zeros((live, B), f32)
        for h in range(2):
            lhs = jnp.concatenate([shifts[c, 2 * h + e, pl.ds(16 * d4, live), :] for e in range(2)], 1)
            rhs = toep[c, :, pl.ds((4 * d4 + 2 * h) * B, 2 * B)]
            part += lax.dot_general(lhs, rhs, (((1,), (1,)), ((), ())), preferred_element_type=f32)
        if live == 256:
            acc += part
        else:
            acc = jnp.concatenate([acc[:live] + part, acc[live:]], 0)
    return acc


PITCH = 136
HALF = 4

def product_blocks(saved_t, shifts, blocks, c, slot):
    for d4 in range(16):
        depth = 256 if d4 < 8 else 128
        for h in range(2):
            m = 4 * d4 + 2 * h
            rhs = jnp.concatenate([shifts[c, 2 * h + e, pl.ds(16 * d4, depth), :] for e in range(2)], 1)
            out = jnp.dot(saved_t[:, :depth], rhs, preferred_element_type=f32)
            for e in range(2):
                blocks[pl.ds(pl.multiple_of((slot * 64 + m + e) * PITCH, 8), B), :] = out[:, e * B:(e + 1) * B]

def fold(blocks, totals, step=32):
    totals[...] = jnp.zeros(totals.shape, f32)
    rows = totals.shape[0]
    k = lax.broadcasted_iota(jnp.int32, (B, 2 * B), 0)
    n = lax.broadcasted_iota(jnp.int32, (B, 2 * B), 1)
    gap = n - k - B

    @pl.loop(0, B // step)
    def _(t):
        lhs, rhs = [], []
        for e in range(step):
            jp = t * step + e
            lhs.append(blocks[pl.ds(jp, rows, stride=PITCH), :].astype(bf16))
            rhs.append(jnp.where(gap == -jp, 1.0, 0.0).astype(bf16))
        totals[...] += jnp.dot(jnp.concatenate(lhs, 1), jnp.concatenate(rhs, 0), preferred_element_type=f32)


def wrap(v, n):
    return jnp.where(v >= n, v - n, v)


def kernel(
    go_hbm, pg_hbm, pre_hbm, val_hbm, filt_hbm, back_ref, taps_ref,
    go, pg, pre, val, g_own, s_own, g_z, s_z, g_all, s_all, c_own, c_xy, c_z, t_own, t_all,
    fpad, toep, grows, srows, shifts, crows, blocks, totals, trows,
    load_sem, z_send, z_recv, xy_send, xy_recv, c_recv, t_send, t_recv,
):
    length = toep.shape[2]
    dp, ctx = lax.axis_index("dp"), lax.axis_index("ctx")
    z = ctx // 8
    plane = ctx - 8 * z
    xl = plane // 4
    y = plane - 4 * xl
    xh = dp // 2
    core = dp - 2 * xh
    x = 2 * xh + xl
    q = plane * 4 + dp
    member = plane * 2 + xh

    loads = [
        pltpu.make_async_copy(a, b, load_sem.at[n])
        for n, (a, b) in enumerate(
            (
                (go_hbm, go), (pg_hbm, pg), (pre_hbm, pre), (val_hbm, val),
                (filt_hbm.at[pl.ds(pl.multiple_of(8 * dp, 8), 8)], fpad.at[:, pl.ds(B, length)]),
            )
        )
    ]
    for load in loads:
        load.start()

    def z_peer(k, back):
        step = ORDER[k] if back else (8 - ORDER[k]) % 8
        return wrap(z + step, 8)

    def chip(x2, y2):
        xh2 = jnp.where(x2 >= 2, 1, 0)
        return (x2 - 2 * xh2) * 4 + y2, xh2

    def each_xy_peer(body):
        @pl.loop(0, 4)
        def _(dy):
            y2 = wrap(y + dy, 4)
            for dx in range(4):
                plane2, xh2 = chip(wrap(x + dx, 4), y2)
                for dc in range(2):
                    dp2 = 2 * xh2 + wrap(core + dc, 2)
                    if dx or dc:
                        body(dp2, z * 8 + plane2, plane2 * 4 + dp2)
                    else:

                        @pl.when(dy > 0)
                        def _():
                            body(dp2, z * 8 + plane2, plane2 * 4 + dp2)

    barrier = pltpu.get_barrier_semaphore()
    for k in range(7):
        pl.semaphore_signal(
            barrier, inc=1, device_id=(dp, z_peer(k, False) * 8 + plane), device_id_type=MESH
        )
    each_xy_peer(
        lambda d, c, q2: pl.semaphore_signal(barrier, inc=1, device_id=(d, c), device_id_type=MESH)
    )

    def elementwise(a, b, out):
        @pl.loop(0, 8)
        def _(there):
            rows = pl.ds(pl.multiple_of(there * 256, 256), 256)
            prod = (a[rows, :].astype(f32) * b[rows, :].astype(f32)).reshape(16, 2, 8, B)
            for n in range(2):
                out[n, there] = prod[:, n].astype(bf16)

    def z_sends(src, dst, t, n):
        return [
            pltpu.make_async_remote_copy(
                src_ref=src.at[n, z_peer(k, False)], dst_ref=dst.at[n, k],
                send_sem=z_send.at[t, n, k], recv_sem=z_recv.at[t, n, k],
                device_id=(dp, z_peer(k, False) * 8 + plane), device_id_type=MESH,
            )
            for k in range(7)
        ]

    def spread(src, dst, t, n):
        @pl.loop(0, 4)
        def _(dy):
            y2 = wrap(y + dy, 4)
            for dx in range(4):
                plane2, xh2 = chip(wrap(x + dx, 4), y2)
                copy = pltpu.make_async_remote_copy(
                    src_ref=src.at[n, :, plane2 * 2 + xh2], dst_ref=dst.at[q],
                    send_sem=xy_send.at[t], recv_sem=xy_recv.at[t],
                    device_id=(2 * xh2 + n, z * 8 + plane2), device_id_type=MESH,
                )
                if dx:
                    copy.start()
                else:
                    pl.when((dy > 0) | (core != n))(copy.start)

    def wait_31(ref, sem):
        part = ref.at[pl.ds(0, 31)]
        pltpu.make_async_copy(part, part, sem).wait()

    loads[0].wait()
    loads[1].wait()
    elementwise(go, pg, g_own)
    pl.semaphore_wait(barrier, 38)
    g_sends = [z_sends(g_own, g_z, 0, n) for n in range(2)]
    s_sends = [z_sends(s_own, s_z, 1, n) for n in range(2)]
    queue = g_sends + s_sends

    def launch(n):
        if n < 4:
            for send in queue[n]:
                send.start()

    def forward(n):
        for send in queue[n]:
            send.wait_recv()
        launch(n + AHEAD)
        if n < 2:
            spread(g_z, g_all, 0, n)
        else:
            spread(s_z, s_all, 1, n - 2)

    for n in range(AHEAD):
        launch(n)
    for n in range(2):
        g_z[n, 7] = g_own[n, z]
    loads[2].wait()
    loads[3].wait()
    elementwise(pre, val, s_own)
    for n in range(2):
        s_z[n, 7] = s_own[n, z]

    loads[4].wait()
    fpad[:, :B] = jnp.zeros((8, B), f32)
    grows[pl.ds(2048, 128), :] = jnp.zeros((128, B), f32)
    shifts[:, :, pl.ds(256, 128), :] = jnp.zeros((8, 4, 128, B), bf16)
    build_filters(fpad, toep, 0, 3)
    forward(0)
    build_filters(fpad, toep, 3, 6)
    forward(1)
    g_all[q] = g_z[core, :, member]
    build_filters(fpad, toep, 6, 8)

    def unpack(slabs, rows):
        for k in range(8):
            there = wrap(z + ORDER[k], 8)
            rows[pl.ds(pl.multiple_of(there * 256, 256), 256), :] = (
                slabs[:, k].astype(f32).reshape(256, B)
            )

    wait_31(g_all, xy_recv.at[0])
    unpack(g_all, grows)

    def correlations(first, last):
        @pl.loop(first, last)
        def _(c):
            shifted(grows, shifts, c)
            crows[pl.ds(c, 256, stride=8), :] = correlate(toep, shifts, c)

    correlations(0, 3)
    forward(2)
    correlations(3, 6)
    forward(3)
    s_all[q] = s_z[core, :, member]
    correlations(6, 8)

    for k in range(8):
        there = wrap(z + ORDER[k], 8)
        c_own[:, k] = (
            crows[pl.ds(pl.multiple_of(there * 256, 256), 256), :].astype(bf16).reshape(32, 8, B)
        )

    def back(d, c, q2):
        pltpu.make_async_remote_copy(
            src_ref=c_own.at[q2], dst_ref=c_xy.at[core, member],
            send_sem=xy_send.at[2], recv_sem=c_recv.at[core],
            device_id=(d, c), device_id_type=MESH,
        ).start()

    each_xy_peer(back)
    c_xy[core, member] = c_own[q]

    c_sends = [
        pltpu.make_async_remote_copy(
            src_ref=c_xy.at[n, :, k], dst_ref=c_z.at[k, n],
            send_sem=z_send.at[2, n, k], recv_sem=z_recv.at[2, n, k],
            device_id=(dp, z_peer(k, True) * 8 + plane), device_id_type=MESH,
        )
        for n in range(2)
        for k in range(7)
    ]

    def part_wait(n, count):
        part = c_xy.at[n, pl.ds(0, count)]
        pltpu.make_async_copy(part, part, c_recv.at[n]).wait()

    def send_back(n):
        pl.when(core == n)(lambda: part_wait(n, 15))
        pl.when(core != n)(lambda: part_wait(n, 16))
        for send in c_sends[7 * n : 7 * n + 7]:
            send.start()
        c_z[7, n] = c_xy[n, :, 7]

    def multiply(first, last, base):
        @pl.loop(first, last, unroll=True)
        def _(c):
            saved_t = srows[pl.ds(c, 256, stride=8), :].T.astype(bf16)
            product_blocks(saved_t, shifts, blocks, c, c - base)

    def sum_up(base):
        fold(blocks, totals)
        for n in range(HALF):
            here = totals[pl.ds(64 * n, 64), pl.ds(B, B)]
            later = totals[pl.ds(64 * n, 64), pl.ds(0, B)]
            later = jnp.concatenate([later[1:], jnp.zeros((1, B), f32)], 0)
            trows[pl.ds(base + n, 64, stride=8), :] = here + later

    wait_31(s_all, xy_recv.at[1])
    unpack(s_all, srows)
    multiply(0, 2, 0)
    send_back(0)
    multiply(2, 4, 0)
    send_back(1)
    sum_up(0)
    multiply(4, 6, 4)
    multiply(6, 8, 4)
    sum_up(4)

    for p in range(4):
        t_own[p] = trows[pl.ds(128 * p, 128), :].astype(bf16).reshape(16, 8, B)
    t_sends = []
    for s in range(1, 4):
        p = wrap(dp + s, 4)
        t_sends.append(
            pltpu.make_async_remote_copy(
                src_ref=t_own.at[p], dst_ref=t_all.at[s],
                send_sem=t_send.at[s - 1], recv_sem=t_recv.at[s - 1],
                device_id=(p, ctx), device_id_type=MESH,
            )
        )
        t_sends[-1].start()
    t_all[0] = t_own[dp]

    for send in c_sends:
        send.wait_recv()
    for k in range(8):
        for n in range(2):
            for m in range(16):
                back_ref[z_peer(k, False), 2 * m + n] = c_z[k, n, m]

    for s in range(4):
        if s:
            t_sends[s - 1].wait_recv()
        rows = pl.ds(pl.multiple_of(8 * wrap(dp + (4 - s) % 4, 4), 8), 8)
        for m in range(16):
            taps_ref[rows, pl.ds(m * B, B)] = t_all[s, m].astype(f32)

    for send in sum(queue, []) + c_sends + t_sends:
        send.wait_send()
    wait_31(g_all, xy_send.at[0])
    wait_31(s_all, xy_send.at[1])
    wait_31(c_own, xy_send.at[2])


def finish_kernel(scale, c, go, pg, pre, val, skip, taps, gp, gv, out):
    skip_t = skip[...].T
    for n in range(8):
        rows = pl.ds(n * B, B)
        gated = (go[rows, :].astype(f32) * pg[rows, :].astype(f32)).astype(bf16).astype(f32)
        summed = c[rows, :].astype(f32) + skip_t[:, n : n + 1] * gated
        gp[rows, :] = (summed * val[rows, :].astype(f32)).astype(bf16)
        gv[rows, :] = (summed * pre[rows, :].astype(f32)).astype(bf16)
    out[...] = taps[...] * scale


def finish(back, go, pg, pre, val, skip, taps, scale):
    rows = pl.BlockSpec((1024, B), lambda n: (n, 0))
    part = pl.BlockSpec((16, taps.shape[1]), lambda n: (n, 0))
    return pl.pallas_call(
        functools.partial(finish_kernel, scale),
        grid=(2,),
        out_shape=(
            jax.ShapeDtypeStruct(go.shape, bf16),
            jax.ShapeDtypeStruct(go.shape, bf16),
            jax.ShapeDtypeStruct(taps.shape, f32),
        ),
        in_specs=[rows] * 5 + [pl.BlockSpec((8, B), lambda n: (n, 0)), part],
        out_specs=(rows, rows, part),
        name="finish",
    )(back, go, pg, pre, val, skip, taps)


def shards(grad_output, post_gate, pre_gate, value_branch, long_filter, skip_weight):
    channels, length = skip_weight.shape[0], long_filter.shape[1]
    vm = pl.BlockSpec(memory_space=pltpu.VMEM)
    own = pltpu.VMEM((channels, B), bf16)
    by_class = pltpu.VMEM((2, 8, 16, 8, B), bf16)
    by_q = pltpu.VMEM((32, 8, 8, B), bf16)
    by_p = pltpu.VMEM((4, 16, 8, B), bf16)
    dma = pltpu.SemaphoreType.DMA
    back, taps = pl.pallas_call(
        kernel,
        out_shape=(
            jax.ShapeDtypeStruct((8, 32, 8, B), bf16),
            jax.ShapeDtypeStruct((32, length // 4), f32),
        ),
        in_specs=[pl.BlockSpec(memory_space=pl.ANY)] * 5,
        out_specs=(vm, vm),
        scratch_shapes=[own] * 4
        + [by_class] * 4
        + [by_q] * 3
        + [pltpu.VMEM((2, 16, 8, 8, B), bf16), pltpu.VMEM((8, 2, 16, 8, B), bf16)]
        + [by_p] * 2
        + [
            pltpu.VMEM((8, length + B), f32),
            pltpu.VMEM((8, B, length), bf16),
            pltpu.VMEM((2048 + 128, B), f32),
            pltpu.VMEM((2048, B), f32),
            pltpu.VMEM((8, 4, 384, B), bf16),
            pltpu.VMEM((2048, B), f32),
            pltpu.VMEM((HALF * 64 * PITCH, B), f32),
            pltpu.VMEM((HALF * 64, 2 * B), f32),
            pltpu.VMEM((512, B), f32),
            dma((5,)),
            dma((3, 2, 7)),
            dma((3, 2, 7)),
            dma((3,)),
            dma((2,)),
            dma((2,)),
            dma((3,)),
            dma((3,)),
        ],
        compiler_params=pltpu.CompilerParams(
            collective_id=0, has_side_effects=True, vmem_limit_bytes=62 << 20
        ),
        name="hyena",
    )(grad_output[0], post_gate[0], pre_gate[0], value_branch[0], long_filter)
    gp, gv, taps = finish(
        back.reshape(channels, B), grad_output[0], post_gate[0], pre_gate[0], value_branch[0],
        skip_weight.reshape(16, B), taps, 1.0 / math.sqrt(4 * length),
    )
    return gp[None], gv[None], taps


def solution(mesh):
    return jax.shard_map(
        shards,
        mesh=mesh,
        in_specs=(P("dp", None, "ctx"),) * 4 + (P("ctx", None), P()),
        out_specs=(P("dp", None, "ctx"), P("dp", None, "ctx"), P("ctx", "dp")),
        check_vma=False,
    )
```

```python
import functools
import math

import jax
import jax.numpy as jnp
from jax import lax
from jax.experimental import pallas as pl
from jax.experimental.pallas import tpu as pltpu
from jax.sharding import PartitionSpec as P

MESH = pl.DeviceIdType.MESH
ORDER = (4, 3, 5, 6, 2, 7, 1, 0)
AHEAD = 2

f32, bf16 = jnp.float32, jnp.bfloat16
B = 128
W = 2048


def row_bits(shape):
    return lax.broadcasted_iota(jnp.int32, shape, 0)


def stagger(v, left):
    width = v.shape[1]
    rows = row_bits(v.shape)
    for bit in (1, 2, 4):
        moved = pltpu.roll(v, (width - bit) if left else bit, 1)
        v = jnp.where((rows & bit) != 0, moved, v)
    return v


def build_filters(fpad, toep, first, last):
    length = toep.shape[2]

    @pl.loop(first, last)
    def _(c):
        @pl.loop(0, length // W)
        def _(w):
            lanes = pl.ds(pl.multiple_of(w * W, W), W + B)
            v = jnp.broadcast_to(fpad[pl.ds(c, 1), lanes], (8, W + B))
            v = stagger(v, False)
            for a in range(0, 16, 2):
                lo = v if a == 0 else pltpu.roll(v, 8 * a, 1)
                hi = pltpu.roll(v, 8 * a + 8, 1)
                both = jnp.concatenate([lo[:, B:], hi[:, B:]], 0).astype(bf16)
                toep[c, pl.ds(8 * a, 16), pl.ds(pl.multiple_of(w * W, W), W)] = both


def shifted(rows, out, c):
    for p in range(4):
        out[c, p, pl.ds(0, 256), :] = rows[pl.ds(c + 32 * p, 256, stride=8), :].astype(bf16)


def correlate(toep, shifts, c):
    acc = jnp.zeros((256, B), f32)
    for d4 in range(16):
        live = 256 - 16 * d4
        part = jnp.zeros((live, B), f32)
        for h in range(2):
            lhs = jnp.concatenate([shifts[c, 2 * h + e, pl.ds(16 * d4, live), :] for e in range(2)], 1)
            rhs = toep[c, :, pl.ds((4 * d4 + 2 * h) * B, 2 * B)]
            part += lax.dot_general(lhs, rhs, (((1,), (1,)), ((), ())), preferred_element_type=f32)
        if live == 256:
            acc += part
        else:
            acc = jnp.concatenate([acc[:live] + part, acc[live:]], 0)
    return acc


PITCH = 136
HALF = 4

def product_blocks(saved_t, shifts, blocks, c, slot):
    for d4 in range(16):
        depth = 256 if d4 < 8 else 128
        for h in range(2):
            m = 4 * d4 + 2 * h
            rhs = jnp.concatenate([shifts[c, 2 * h + e, pl.ds(16 * d4, depth), :] for e in range(2)], 1)
            out = jnp.dot(saved_t[:, :depth], rhs, preferred_element_type=f32)
            for e in range(2):
                blocks[pl.ds(pl.multiple_of((slot * 64 + m + e) * PITCH, 8), B), :] = out[:, e * B:(e + 1) * B]

def fold(blocks, totals, step=32):
    totals[...] = jnp.zeros(totals.shape, f32)
    rows = totals.shape[0]
    k = lax.broadcasted_iota(jnp.int32, (B, 2 * B), 0)
    n = lax.broadcasted_iota(jnp.int32, (B, 2 * B), 1)
    gap = n - k - B

    @pl.loop(0, B // step)
    def _(t):
        lhs, rhs = [], []
        for e in range(step):
            jp = t * step + e
            lhs.append(blocks[pl.ds(jp, rows, stride=PITCH), :].astype(bf16))
            rhs.append(jnp.where(gap == -jp, 1.0, 0.0).astype(bf16))
        totals[...] += jnp.dot(jnp.concatenate(lhs, 1), jnp.concatenate(rhs, 0), preferred_element_type=f32)


def wrap(v, n):
    return jnp.where(v >= n, v - n, v)


def kernel(
    go_hbm, pg_hbm, pre_hbm, val_hbm, filt_hbm, back_ref, taps_ref,
    go, pg, pre, val, g_own, s_own, g_z, s_z, g_all, s_all, c_own, c_xy, c_z, t_own, t_all,
    fpad, toep, grows, srows, shifts, crows, blocks, totals, trows,
    load_sem, z_send, z_recv, xy_send, xy_recv, c_recv, t_send, t_recv,
):
    length = toep.shape[2]
    dp, ctx = lax.axis_index("dp"), lax.axis_index("ctx")
    z = ctx // 8
    plane = ctx - 8 * z
    xl = plane // 4
    y = plane - 4 * xl
    xh = dp // 2
    core = dp - 2 * xh
    x = 2 * xh + xl
    q = plane * 4 + dp
    member = plane * 2 + xh

    loads = [
        pltpu.make_async_copy(a, b, load_sem.at[n])
        for n, (a, b) in enumerate(
            (
                (go_hbm, go), (pg_hbm, pg), (pre_hbm, pre), (val_hbm, val),
                (filt_hbm.at[pl.ds(pl.multiple_of(8 * dp, 8), 8)], fpad.at[:, pl.ds(B, length)]),
            )
        )
    ]
    for load in loads:
        load.start()

    def z_peer(k, back):
        step = ORDER[k] if back else (8 - ORDER[k]) % 8
        return wrap(z + step, 8)

    def chip(x2, y2):
        xh2 = jnp.where(x2 >= 2, 1, 0)
        return (x2 - 2 * xh2) * 4 + y2, xh2

    def each_xy_peer(body):
        @pl.loop(0, 4)
        def _(dy):
            y2 = wrap(y + dy, 4)
            for dx in range(4):
                plane2, xh2 = chip(wrap(x + dx, 4), y2)
                for dc in range(2):
                    dp2 = 2 * xh2 + wrap(core + dc, 2)
                    if dx or dc:
                        body(dp2, z * 8 + plane2, plane2 * 4 + dp2)
                    else:

                        @pl.when(dy > 0)
                        def _():
                            body(dp2, z * 8 + plane2, plane2 * 4 + dp2)

    barrier = pltpu.get_barrier_semaphore()
    for k in range(7):
        pl.semaphore_signal(
            barrier, inc=1, device_id=(dp, z_peer(k, False) * 8 + plane), device_id_type=MESH
        )
    each_xy_peer(
        lambda d, c, q2: pl.semaphore_signal(barrier, inc=1, device_id=(d, c), device_id_type=MESH)
    )

    def elementwise(a, b, out):
        @pl.loop(0, 8)
        def _(there):
            rows = pl.ds(pl.multiple_of(there * 256, 256), 256)
            prod = (a[rows, :].astype(f32) * b[rows, :].astype(f32)).reshape(16, 2, 8, B)
            for n in range(2):
                out[n, there] = prod[:, n].astype(bf16)

    def z_sends(src, dst, t, n):
        return [
            pltpu.make_async_remote_copy(
                src_ref=src.at[n, z_peer(k, False)], dst_ref=dst.at[n, k],
                send_sem=z_send.at[t, n, k], recv_sem=z_recv.at[t, n, k],
                device_id=(dp, z_peer(k, False) * 8 + plane), device_id_type=MESH,
            )
            for k in range(7)
        ]

    def spread(src, dst, t, n):
        @pl.loop(0, 4)
        def _(dy):
            y2 = wrap(y + dy, 4)
            for dx in range(4):
                plane2, xh2 = chip(wrap(x + dx, 4), y2)
                copy = pltpu.make_async_remote_copy(
                    src_ref=src.at[n, :, plane2 * 2 + xh2], dst_ref=dst.at[q],
                    send_sem=xy_send.at[t], recv_sem=xy_recv.at[t],
                    device_id=(2 * xh2 + n, z * 8 + plane2), device_id_type=MESH,
                )
                if dx:
                    copy.start()
                else:
                    pl.when((dy > 0) | (core != n))(copy.start)

    def wait_31(ref, sem):
        part = ref.at[pl.ds(0, 31)]
        pltpu.make_async_copy(part, part, sem).wait()

    loads[0].wait()
    loads[1].wait()
    elementwise(go, pg, g_own)
    pl.semaphore_wait(barrier, 38)
    g_sends = [z_sends(g_own, g_z, 0, n) for n in range(2)]
    s_sends = [z_sends(s_own, s_z, 1, n) for n in range(2)]
    queue = g_sends + s_sends

    def launch(n):
        if n < 4:
            for send in queue[n]:
                send.start()

    def forward(n):
        for send in queue[n]:
            send.wait_recv()
        launch(n + AHEAD)
        if n < 2:
            spread(g_z, g_all, 0, n)
        else:
            spread(s_z, s_all, 1, n - 2)

    for n in range(AHEAD):
        launch(n)
    for n in range(2):
        g_z[n, 7] = g_own[n, z]
    loads[2].wait()
    loads[3].wait()
    elementwise(pre, val, s_own)
    for n in range(2):
        s_z[n, 7] = s_own[n, z]

    loads[4].wait()
    fpad[:, :B] = jnp.zeros((8, B), f32)
    grows[pl.ds(2048, 128), :] = jnp.zeros((128, B), f32)
    shifts[:, :, pl.ds(256, 128), :] = jnp.zeros((8, 4, 128, B), bf16)
    build_filters(fpad, toep, 0, 3)
    forward(0)
    build_filters(fpad, toep, 3, 6)
    forward(1)
    g_all[q] = g_z[core, :, member]
    build_filters(fpad, toep, 6, 8)

    def unpack(slabs, rows):
        for k in range(8):
            there = wrap(z + ORDER[k], 8)
            rows[pl.ds(pl.multiple_of(there * 256, 256), 256), :] = (
                slabs[:, k].astype(f32).reshape(256, B)
            )

    wait_31(g_all, xy_recv.at[0])
    unpack(g_all, grows)

    def correlations(first, last):
        @pl.loop(first, last)
        def _(c):
            shifted(grows, shifts, c)
            crows[pl.ds(c, 256, stride=8), :] = correlate(toep, shifts, c)

    correlations(0, 3)
    forward(2)
    correlations(3, 6)
    forward(3)
    s_all[q] = s_z[core, :, member]
    correlations(6, 8)

    for k in range(8):
        there = wrap(z + ORDER[k], 8)
        c_own[:, k] = (
            crows[pl.ds(pl.multiple_of(there * 256, 256), 256), :].astype(bf16).reshape(32, 8, B)
        )

    def back(d, c, q2):
        pltpu.make_async_remote_copy(
            src_ref=c_own.at[q2], dst_ref=c_xy.at[core, member],
            send_sem=xy_send.at[2], recv_sem=c_recv.at[core],
            device_id=(d, c), device_id_type=MESH,
        ).start()

    each_xy_peer(back)
    c_xy[core, member] = c_own[q]

    c_sends = [
        pltpu.make_async_remote_copy(
            src_ref=c_xy.at[n, :, k], dst_ref=c_z.at[k, n],
            send_sem=z_send.at[2, n, k], recv_sem=z_recv.at[2, n, k],
            device_id=(dp, z_peer(k, True) * 8 + plane), device_id_type=MESH,
        )
        for n in range(2)
        for k in range(7)
    ]

    def part_wait(n, count):
        part = c_xy.at[n, pl.ds(0, count)]
        pltpu.make_async_copy(part, part, c_recv.at[n]).wait()

    def send_back(n):
        pl.when(core == n)(lambda: part_wait(n, 15))
        pl.when(core != n)(lambda: part_wait(n, 16))
        for send in c_sends[7 * n : 7 * n + 7]:
            send.start()
        c_z[7, n] = c_xy[n, :, 7]

    def multiply(first, last, base):
        @pl.loop(first, last, unroll=True)
        def _(c):
            saved_t = srows[pl.ds(c, 256, stride=8), :].T.astype(bf16)
            product_blocks(saved_t, shifts, blocks, c, c - base)

    def sum_up(base):
        fold(blocks, totals)
        for n in range(HALF):
            here = totals[pl.ds(64 * n, 64), pl.ds(B, B)]
            later = totals[pl.ds(64 * n, 64), pl.ds(0, B)]
            later = jnp.concatenate([later[1:], jnp.zeros((1, B), f32)], 0)
            trows[pl.ds(base + n, 64, stride=8), :] = here + later

    wait_31(s_all, xy_recv.at[1])
    unpack(s_all, srows)
    multiply(0, 2, 0)
    send_back(0)
    multiply(2, 4, 0)
    send_back(1)
    sum_up(0)
    multiply(4, 6, 4)
    multiply(6, 8, 4)
    sum_up(4)

    for p in range(4):
        t_own[p] = trows[pl.ds(128 * p, 128), :].astype(bf16).reshape(16, 8, B)
    t_sends = []
    for s in range(1, 4):
        p = wrap(dp + s, 4)
        t_sends.append(
            pltpu.make_async_remote_copy(
                src_ref=t_own.at[p], dst_ref=t_all.at[s],
                send_sem=t_send.at[s - 1], recv_sem=t_recv.at[s - 1],
                device_id=(p, ctx), device_id_type=MESH,
            )
        )
        t_sends[-1].start()
    t_all[0] = t_own[dp]

    for k in range(8):
        if k < 7:
            c_sends[k].wait_recv()
            c_sends[7 + k].wait_recv()
        there = z_peer(k, False)
        for n in range(2):
            for m in range(16):
                back_ref[there, 2 * m + n] = c_z[k, n, m]

    for s in range(4):
        if s:
            t_sends[s - 1].wait_recv()
        rows = pl.ds(pl.multiple_of(8 * wrap(dp + (4 - s) % 4, 4), 8), 8)
        for m in range(16):
            taps_ref[rows, pl.ds(m * B, B)] = t_all[s, m].astype(f32)

    for send in sum(queue, []) + c_sends + t_sends:
        send.wait_send()
    wait_31(g_all, xy_send.at[0])
    wait_31(s_all, xy_send.at[1])
    wait_31(c_own, xy_send.at[2])


def finish_kernel(scale, c, go, pg, pre, val, skip, taps, gp, gv, out):
    skip_t = skip[...].T
    for n in range(8):
        rows = pl.ds(n * B, B)
        gated = (go[rows, :].astype(f32) * pg[rows, :].astype(f32)).astype(bf16).astype(f32)
        summed = c[rows, :].astype(f32) + skip_t[:, n : n + 1] * gated
        gp[rows, :] = (summed * val[rows, :].astype(f32)).astype(bf16)
        gv[rows, :] = (summed * pre[rows, :].astype(f32)).astype(bf16)
    out[...] = taps[...] * scale


def finish(back, go, pg, pre, val, skip, taps, scale):
    rows = pl.BlockSpec((1024, B), lambda n: (n, 0))
    part = pl.BlockSpec((16, taps.shape[1]), lambda n: (n, 0))
    return pl.pallas_call(
        functools.partial(finish_kernel, scale),
        grid=(2,),
        out_shape=(
            jax.ShapeDtypeStruct(go.shape, bf16),
            jax.ShapeDtypeStruct(go.shape, bf16),
            jax.ShapeDtypeStruct(taps.shape, f32),
        ),
        in_specs=[rows] * 5 + [pl.BlockSpec((8, B), lambda n: (n, 0)), part],
        out_specs=(rows, rows, part),
        name="finish",
    )(back, go, pg, pre, val, skip, taps)


def shards(grad_output, post_gate, pre_gate, value_branch, long_filter, skip_weight):
    channels, length = skip_weight.shape[0], long_filter.shape[1]
    vm = pl.BlockSpec(memory_space=pltpu.VMEM)
    own = pltpu.VMEM((channels, B), bf16)
    by_class = pltpu.VMEM((2, 8, 16, 8, B), bf16)
    by_q = pltpu.VMEM((32, 8, 8, B), bf16)
    by_p = pltpu.VMEM((4, 16, 8, B), bf16)
    dma = pltpu.SemaphoreType.DMA
    back, taps = pl.pallas_call(
        kernel,
        out_shape=(
            jax.ShapeDtypeStruct((8, 32, 8, B), bf16),
            jax.ShapeDtypeStruct((32, length // 4), f32),
        ),
        in_specs=[pl.BlockSpec(memory_space=pl.ANY)] * 5,
        out_specs=(vm, vm),
        scratch_shapes=[own] * 4
        + [by_class] * 4
        + [by_q] * 3
        + [pltpu.VMEM((2, 16, 8, 8, B), bf16), pltpu.VMEM((8, 2, 16, 8, B), bf16)]
        + [by_p] * 2
        + [
            pltpu.VMEM((8, length + B), f32),
            pltpu.VMEM((8, B, length), bf16),
            pltpu.VMEM((2048 + 128, B), f32),
            pltpu.VMEM((2048, B), f32),
            pltpu.VMEM((8, 4, 384, B), bf16),
            pltpu.VMEM((2048, B), f32),
            pltpu.VMEM((HALF * 64 * PITCH, B), f32),
            pltpu.VMEM((HALF * 64, 2 * B), f32),
            pltpu.VMEM((512, B), f32),
            dma((5,)),
            dma((3, 2, 7)),
            dma((3, 2, 7)),
            dma((3,)),
            dma((2,)),
            dma((2,)),
            dma((3,)),
            dma((3,)),
        ],
        compiler_params=pltpu.CompilerParams(
            collective_id=0, has_side_effects=True, vmem_limit_bytes=62 << 20
        ),
        name="hyena",
    )(grad_output[0], post_gate[0], pre_gate[0], value_branch[0], long_filter)
    gp, gv, taps = finish(
        back.reshape(channels, B), grad_output[0], post_gate[0], pre_gate[0], value_branch[0],
        skip_weight.reshape(16, B), taps, 1.0 / math.sqrt(4 * length),
    )
    return gp[None], gv[None], taps


def solution(mesh):
    return jax.shard_map(
        shards,
        mesh=mesh,
        in_specs=(P("dp", None, "ctx"),) * 4 + (P("ctx", None), P()),
        out_specs=(P("dp", None, "ctx"), P("dp", None, "ctx"), P("ctx", "dp")),
        check_vma=False,
    )
```
